256 devices in a mesh: rep: 8 (over y_lo, x), fsdp: 32 (over z, y_hi, core).
Axes of the slice: x: 4, y: 4 (y_hi: 2, y_lo: 2; y = y_hi * 2 + y_lo), z: 8, core: 2. Of those that a mesh axis runs over, the one named last changes fastest.
Arguments:
- activations: bfloat16 [8, 8192, 8192], P('rep', 'fsdp'), may hold values from -6 to 6
- weights: bfloat16 [8, 8192, 512], P('rep', 'fsdp'), may hold values from -6 to 6
- momentum: float32 [8, 8192, 512], P('rep', 'fsdp'), may hold values from -6 to 6
- cotangent: bfloat16 [8, 8192, 512], P('rep', 'fsdp'), may hold values from -6 to 6
- step_index: int32 [1], replicated, may hold values from 0 to 999
Outputs:
- values_out: bfloat16 [8, 8192, 512], P('rep', 'fsdp')
- input_grad: bfloat16 [8, 8192, 8192], P('rep', 'fsdp')
- new_weights: bfloat16 [8, 8192, 512], P('rep', 'fsdp')
- new_momentum: float32 [8, 8192, 512], P('rep', 'fsdp')
The draws below stay inside these ranges and needn't reach their ends.
All inputs are finite; a program needn't handle non-finite values.
Results may differ from the reference program's by a relative error of at most 0.015.
Values may be sent and summed in bfloat16 or wider, within the bound.
No kernel may reach another device: no remote copies, remote signals or barrier semaphores. Data moves between devices by JAX's collectives and lax.ppermute only.
A program may use at most 128 MiB of HBM per device.

```python
import jax
import jax.numpy as jnp
from jax import lax

D = 8192
KV = 512
TOK_DEV = 256
GROUP_TOK = 8192
N_REP = 8
N_FSDP = 32


def strengthened(entries, own_key, source, target, parts, factor):
    def block_of(dim):
        return (jnp.arange(entries.shape[dim]) // (entries.shape[dim] // parts)).reshape((-1,) + (1,) * (entries.ndim - 1 - dim))

    near = jax.random.permutation(own_key, parts)[block_of(target)]
    far = (block_of(target) + parts // 2) % parts
    return jnp.where((block_of(source) == near) | (block_of(source) == far), factor * entries, entries)


def steps_of(stream_key, dims, cuts, smallest, top_value):
    def one(axis_at, shards_of):
        steps = jax.random.uniform(jax.random.fold_in(jax.random.fold_in(stream_key, 6), axis_at), (shards_of,), jnp.float32, smallest / len(cuts), top_value / len(cuts))
        return jnp.repeat(jnp.exp(steps), dims[axis_at] // shards_of).reshape((-1,) + (1,) * (len(dims) - axis_at - 1))

    loudness = one(*cuts[0])
    for cut in cuts[1:]:
        loudness = loudness * one(*cut)
    return loudness


def noise(own_key, extent, width, reach, shards=(), held_as=jnp.bfloat16):
    drawn = jax.random.normal(own_key, extent, jnp.float32) * width
    if len(shards) > 0:
        drawn = steps_of(own_key, extent, shards, -0.22, 0.18) * drawn
    return jnp.clip(drawn, min=-reach, max=reach).astype(held_as)


def noise_with(rng, extent, spread, reach, pieces, heavy, kind=jnp.bfloat16):
    values = spread * jax.random.normal(rng, extent, jnp.float32)
    if pieces:
        values = values * steps_of(rng, extent, pieces, -0.22, 0.18)
    return jnp.clip(strengthened(values, jax.random.fold_in(rng, 3), *heavy), -reach, reach).astype(kind)


def setup_inputs(seed: int = 0) -> dict:
    arg_keys = jax.random.split(jax.random.key(seed), 6)
    activations = noise_with(arg_keys[0], (N_REP, GROUP_TOK, D), 1.0, 6.0, ((0, 8), (1, 32)), (1, 2, 32, 2.75))
    weights = noise(arg_keys[1], (N_REP, D, KV), 1.0, 6.0, ((0, 8), (1, 32)))
    momentum = noise(arg_keys[2], (N_REP, D, KV), 1.0, 6.0, ((0, 8), (1, 32)), jnp.float32)
    cotangent = noise(arg_keys[3], (N_REP, GROUP_TOK, KV), 1.0, 6.0, ((0, 8), (1, 32)))
    step_index = jax.random.randint(arg_keys[4], (1,), 0, 1000).astype(jnp.int32)
    return dict(activations=activations, weights=weights, momentum=momentum, cotangent=cotangent, step_index=step_index)


def one_group(args):
    acts, weight, moment, cot, rate = args
    scale = 1.0 / jnp.sqrt(jnp.float32(D))
    values = (jnp.dot(acts, weight, preferred_element_type=jnp.float32) * scale).astype(jnp.bfloat16)
    ingrad = (lax.dot_general(cot, weight, (((1,), (1,)), ((), ())), preferred_element_type=jnp.float32) * scale).astype(jnp.bfloat16)
    blocks_a = acts.reshape(N_FSDP, TOK_DEV, D)
    blocks_c = cot.reshape(N_FSDP, TOK_DEV, KV)

    def add_block(total, pair):
        block_a, block_c = pair
        part = lax.dot_general(block_a, block_c, (((0,), (0,)), ((), ())), preferred_element_type=jnp.float32) * scale
        return (total + part.astype(jnp.bfloat16).astype(jnp.float32), None)
    grad, _ = lax.scan(add_block, jnp.zeros((D, KV), jnp.float32), (blocks_a, blocks_c))
    moved = 0.9 * moment + grad
    stepped = (weight.astype(jnp.float32) - rate * moved).astype(jnp.bfloat16)
    return (values, ingrad, stepped, moved)

def reference(activations, weights, momentum, cotangent, step_index):
    step_float = step_index[0].astype(jnp.float32)
    rate = 0.1 * (0.5 + 0.5 * jnp.cos(jnp.float32(3.141592653589793) * step_float / 1000.0))
    rates = jnp.broadcast_to(rate, (N_REP,))
    values, ingrad, stepped, moved = lax.map(one_group, (activations, weights, momentum, cotangent, rates))
    bits = int(N_REP).bit_length() - 1
    bit_pick = (step_index[0] % bits).astype(jnp.int32)
    groups = jnp.arange(N_REP, dtype=jnp.int32)
    partner = jnp.bitwise_xor(groups, jnp.left_shift(jnp.int32(1), bit_pick)).astype(jnp.int32)
    other_w = jnp.take(stepped, partner, axis=0)
    other_m = jnp.take(moved, partner, axis=0)
    new_w = ((stepped.astype(jnp.float32) + other_w.astype(jnp.float32)) * 0.5).astype(jnp.bfloat16)
    new_m = (moved + other_m) * 0.5
    return (values, ingrad, new_w, new_m)
```

```python
from functools import partial

import jax
import jax.numpy as jnp
from jax import lax
from jax.experimental import pallas as pl
from jax.experimental.pallas import tpu as pltpu
from jax.sharding import PartitionSpec as P

BF = jnp.bfloat16
F32 = jnp.float32
Z = 8
HALF = 128
SHARD = 256
VMEM_LIMIT = 40 * 2**20


def send(value, move, axis="fsdp"):
    pairs = [(source, move(source)) for source in range(lax.axis_size(axis))]
    return lax.ppermute(value, axis, pairs)


def up(value):
    return send(value, lambda f: (f + 4) % 32)


def down(value):
    return send(value, lambda f: (f - 4) % 32)


def y_swap(value):
    return send(value, lambda f: f ^ 2)


def core_swap(value):
    return send(value, lambda f: f ^ 1)


def cat(*parts):
    return jnp.concatenate(parts, axis=0)


def add(*parts):
    total = parts[0].astype(F32)
    for part in parts[1:]:
        total = total + part.astype(F32)
    return total.astype(BF)


def partials_kernel(where, own_acts, got_acts, own_cot, got_cot, out, *, scale):
    total = lax.dot_general(
        own_acts[...], own_cot[...], (((0,), (0,)), ((), ())), preferred_element_type=F32
    )
    total += lax.dot_general(
        got_acts[...], got_cot[...], (((0,), (0,)), ((), ())), preferred_element_type=F32
    )
    out[...] = (total * scale).astype(BF)


def partials(where, acts, got_acts, cot, got_cot, scale):
    def place(i, where):
        z = lax.rem(where[0] + i // 2, Z)
        y = lax.rem(where[1] + i, 2)
        return z * 2 + y

    return pl.pallas_call(
        partial(partials_kernel, scale=scale),
        grid_spec=pltpu.PrefetchScalarGridSpec(
            num_scalar_prefetch=1,
            grid=(16,),
            in_specs=[
                pl.BlockSpec((SHARD, SHARD), lambda i, w: (0, place(i, w) * 2 + w[2])),
                pl.BlockSpec((SHARD, SHARD), lambda i, w: (0, place(i, w))),
                pl.BlockSpec((SHARD, 512), lambda i, w: (0, 0)),
                pl.BlockSpec((SHARD, 512), lambda i, w: (0, 0)),
            ],
            out_specs=pl.BlockSpec((SHARD, 512), lambda i, w: (i, 0)),
        ),
        out_shape=jax.ShapeDtypeStruct((16 * SHARD, 512), BF),
        compiler_params=pltpu.CompilerParams(vmem_limit_bytes=VMEM_LIMIT),
        cost_estimate=pl.CostEstimate(
            flops=2 * 4096 * 512 * 512, bytes_accessed=9 * 2**20, transcendentals=0
        ),
    )(where, acts, got_acts, cot, got_cot)


def products_kernel(where, *refs, plan, n_pieces, first, last, scale):
    pieces = refs[:n_pieces]
    acts, cot, *rest = refs[n_pieces:]
    if not first:
        total_in, _, *rest = rest
    ingrad, total, block = rest
    step = pl.program_id(0)
    n = len(plan)
    for i, entry in enumerate(plan):

        @pl.when(step == i)
        def _(entry=entry):
            for y, core, row, piece, start, rows in entry:
                y_at = lax.rem(where[n] + y, 2)
                c_at = lax.rem(where[n + 1] + core, 2)
                at = (y_at * 2 + c_at) * SHARD + row
                block[pl.ds(pl.multiple_of(at, 64), rows), :] = pieces[piece][start : start + rows, :]

    part = jnp.dot(acts[...], block[...], preferred_element_type=F32)
    ingrad[...] = (
        lax.dot_general(cot[...], block[...], (((1,), (1,)), ((), ())), preferred_element_type=F32) * scale
    ).astype(BF)

    if first:

        @pl.when(step == 0)
        def _():
            total[...] = part

        @pl.when(step > 0)
        def _():
            total[...] += part
    else:

        @pl.when(step == 0)
        def _():
            total[...] = total_in[...] + part

        @pl.when(step > 0)
        def _():
            total[...] += part

    if last:

        @pl.when(step == n - 1)
        def _():
            total[...] = total[...] * scale


def products(where, plan, pieces, acts, cot, carry, last, scale):
    n = len(plan)
    first = carry is None
    whole = lambda a: pl.BlockSpec(a.shape, lambda i, w: (0, 0))
    wide = pl.BlockSpec((SHARD, 1024), lambda i, w: (0, w[i]))
    held = pl.BlockSpec((SHARD, 512), lambda i, w: (0, 0))
    in_specs = [whole(p) for p in pieces] + [wide, held]
    args = list(pieces) + [acts, cot]
    aliases = {}
    if not first:
        ingrad, total = carry
        in_specs += [held, pl.BlockSpec(memory_space=pl.ANY)]
        args += [total, ingrad]
        aliases = {len(args): 0}
    return pl.pallas_call(
        partial(products_kernel, plan=plan, n_pieces=len(pieces), first=first, last=last, scale=scale),
        grid_spec=pltpu.PrefetchScalarGridSpec(
            num_scalar_prefetch=1,
            grid=(n,),
            in_specs=in_specs,
            out_specs=[wide, held],
            scratch_shapes=[pltpu.VMEM((1024, 512), BF)],
        ),
        out_shape=[
            jax.ShapeDtypeStruct((SHARD, 8192), BF),
            jax.ShapeDtypeStruct((SHARD, 512), F32),
        ],
        input_output_aliases=aliases,
        compiler_params=pltpu.CompilerParams(vmem_limit_bytes=VMEM_LIMIT),
        cost_estimate=pl.CostEstimate(
            flops=n * 4 * SHARD * 1024 * 512, bytes_accessed=n * 2 * 2**20, transcendentals=0
        ),
    )(where, *args)


def both(own_piece, sib_piece, sib_start, y, spans):
    rows = []
    for row, start, count in spans:
        rows.append((y, 0, row, own_piece, start, count))
        rows.append((y, 1, row, sib_piece, sib_start + start, count))
    return rows


def per_device(activations, weights, momentum, cotangent, step_index):
    acts, cot, w = activations[0], cotangent[0], weights[0]
    scale = 1.0 / (8192.0**0.5)
    me = lax.axis_index("fsdp")
    z, y, core = me // 4, (me // 2) % 2, me % 2
    int32 = lambda *v: jnp.stack([jnp.asarray(x, jnp.int32) for x in v])
    low, high = slice(0, HALF), slice(HALF, SHARD)
    rest = slice(SHARD, SHARD + HALF)

    u1, d1 = up(w), down(w)
    y0 = y_swap(w)

    blocks = acts.reshape(SHARD, 16, 2, SHARD)
    give = lax.dynamic_index_in_dim(blocks, 1 - core, 2, keepdims=False).reshape(SHARD, 4096)
    got_acts, got_cot = core_swap(give), core_swap(cot)
    part = partials(int32(z, y, core), acts, got_acts, cot, got_cot, scale)

    def own(d):
        at = (d % Z) * 2 * SHARD
        return part[at : at + SHARD]

    def other(d):
        at = (d % Z) * 2 * SHARD + SHARD
        return part[at : at + SHARD]

    u2, d2 = up(cat(u1, y0[high])), down(cat(d1, y0[high]))
    y1 = y_swap(cat(u1[low], d1[low]))
    c1 = core_swap(cat(w, u1, d1, y0))

    su1, sd1 = up(other(4)[128:192]), down(other(4)[192:256])
    order1, order2 = (4, 3, -3), (2, -2, 1, -1, 0)
    s_y1 = y_swap(cat(*[other(d)[low] for d in order1]))
    s_y2 = y_swap(cat(*[other(d)[low] for d in order2]))
    from_y = {}
    for group, arrived in ((order1, s_y1), (order2, s_y2)):
        for i, d in enumerate(group):
            from_y[d] = arrived[i * HALF : (i + 1) * HALF]

    su2 = up(cat(add(own(4)[low], from_y[4]), add(other(3)[128:192], su1), other(3)[192:256]))
    sd2 = down(cat(own(4)[high], other(-3)[128:192], add(other(-3)[192:256], sd1)))

    u3, d3 = up(u2), down(d2)
    y2 = y_swap(cat(u2[low], d2[low]))
    c2 = core_swap(cat(u2, d2, y1))

    su3 = up(cat(add(own(3)[low], from_y[3], su2[low]), own(3)[high], add(other(2)[high], su2[high])))
    sd3 = down(cat(add(own(-3)[low], from_y[-3]), add(own(-3)[high], sd2[low]), add(other(-2)[high], sd2[high])))

    u4, d4 = up(cat(u3[low], u3[rest])), down(cat(d3[high], d3[rest]))
    y3 = y_swap(cat(u3[low], d3[low]))
    c3 = core_swap(cat(u3, d3, y2))

    def fourth(d, arrived):
        return cat(
            add(own(2 * d)[low], from_y[2 * d], arrived[low]),
            add(own(2 * d)[high], arrived[high]),
            add(other(d)[high], arrived[rest]),
        )

    su4, sd4 = up(fourth(1, su3)), down(fourth(-1, sd3))

    u5, d5 = up(u4[128:192]), down(d4[192:256])
    y4 = y_swap(u4[low])
    c4 = core_swap(cat(u4, d4, y3))

    def fifth(d, arrived):
        return cat(
            add(own(d)[low], from_y[d], arrived[low]),
            add(own(d)[high], arrived[high]),
        )

    su5, sd5 = up(fifth(1, su4)), down(fifth(-1, sd4))
    s_y3 = y_swap(add(other(0)[high], su4[rest], sd4[rest]))
    grad = (own(0).astype(F32) + su5.astype(F32) + sd5.astype(F32)) + cat(from_y[0], s_y3).astype(F32)
    c5 = core_swap(cat(y4, u5, d5))

    bits = lax.axis_size("rep").bit_length() - 1
    step_float = step_index[0].astype(F32)
    rate = 0.1 * (0.5 + 0.5 * jnp.cos(jnp.float32(3.141592653589793) * step_float / 1000.0))
    pick = step_index[0] % bits

    def from_partner(value):
        found = [send(value, lambda r, bit=bit: r ^ (1 << bit), "rep") for bit in range(bits)]
        chosen = found[-1]
        for bit in range(bits - 1):
            chosen = jnp.where(pick == bit, found[bit], chosen)
        return chosen.astype(F32)

    moved = 0.9 * momentum[0] + grad
    other_w = from_partner(w)
    other_m = from_partner(moved.astype(BF))
    stepped = (w.astype(F32) - rate * moved).astype(BF).astype(F32)
    other_s = (other_w - rate * other_m).astype(BF).astype(F32)
    new_w = ((stepped + other_s) * 0.5).astype(BF)
    new_m = (moved + other_m) * 0.5

    full = ((0, 0, SHARD),)
    zs = lambda *ds: int32(*[(z + d) % Z for d in ds], y, core)

    def arrived(dist, u, c, u_at, yk, y_at, c_y, c_y_at, next_u, next_c, next_at):
        return (
            both(u, c, u_at, 0, full)
            + [(1, 0, 0, yk, y_at, HALF), (1, 1, 0, c_y, c_y_at + y_at, HALF)]
            + [(1, 0, HALF, next_u, SHARD, HALF), (1, 1, HALF, next_c, next_at + SHARD, HALF)]
        )

    here = both(0, 4, 0, 0, full) + both(3, 4, 768, 1, full)
    carry = products(
        zs(0, -1, 1),
        (
            here,
            arrived(-1, 1, 4, 256, 7, 0, 8, 768, 5, 8, 0),
            arrived(1, 2, 4, 512, 7, 128, 8, 768, 6, 8, 384),
        ),
        (w, u1, d1, y0, c1, u2, d2, y1, c2),
        acts, cot, None, False, scale,
    )
    carry = products(
        zs(-2, 2),
        (
            arrived(-2, 0, 2, 0, 3, 0, 6, 768, 4, 6, 0),
            arrived(2, 1, 2, 384, 3, 128, 6, 768, 5, 6, 384),
        ),
        (u2, d2, c2, y2, u3, d3, c3),
        acts, cot, carry, False, scale,
    )

    def third(u, u_at, y_at, next_u, next_at):
        return (
            both(u, 2, u_at, 0, full)
            + [(1, 0, 0, 3, y_at, HALF), (1, 1, 0, 6, 512 + y_at, HALF)]
            + [(1, 0, HALF, next_u, HALF, HALF), (1, 1, HALF, 6, next_at + HALF, HALF)]
        )

    carry = products(
        zs(-3, 3),
        (third(0, 0, 0, 4, 0), third(1, 384, 128, 5, 256)),
        (u3, d3, c3, y3, u4, d4, c4),
        acts, cot, carry, False, scale,
    )
    ingrad, total = products(
        zs(4),
        (
            both(0, 2, 0, 0, ((0, 0, HALF),))
            + both(1, 2, 256, 0, ((HALF, 0, HALF),))
            + both(3, 6, 0, 1, ((0, 0, HALF),))
            + both(4, 6, 128, 1, ((HALF, 0, 64),))
            + both(5, 6, 192, 1, ((192, 0, 64),)),
        ),
        (u4, d4, c4, y4, u5, d5, c5),
        acts, cot, carry, True, scale,
    )
    return (total.astype(BF)[None], ingrad[None], new_w[None], new_m[None])


def solution(mesh):
    rows = P("rep", "fsdp", None)
    return jax.shard_map(
        per_device,
        mesh=mesh,
        in_specs=(rows, rows, rows, rows, P()),
        out_specs=(rows, rows, rows, rows),
        check_vma=False,
    )
```

```python
from functools import partial

import jax
import jax.numpy as jnp
from jax import lax
from jax.experimental import pallas as pl
from jax.experimental.pallas import tpu as pltpu
from jax.sharding import PartitionSpec as P

BF = jnp.bfloat16
F32 = jnp.float32
Z = 8
HALF = 128
SHARD = 256
KV = 512
ORDER = (4, 3, -3, 2, -2, 1, -1, 0)
MIB = 2**20
Y, CORE, PICK = 8, 9, 10
TOKEN = pl.BlockSpec((8, 128), lambda *_: (0, 0))
TOKEN_SHAPE = jax.ShapeDtypeStruct((8, 128), F32)


def send(value, move, axis="fsdp"):
    pairs = [(source, move(source)) for source in range(lax.axis_size(axis))]
    return lax.ppermute(value, axis, pairs)


def up(value):
    return send(value, lambda f: (f + 4) % 32)


def down(value):
    return send(value, lambda f: (f - 4) % 32)


def y_swap(value):
    return send(value, lambda f: f ^ 2)


def core_swap(value):
    return send(value, lambda f: f ^ 1)


def from_partner(value, *, bit):
    return send(value, lambda r: r ^ (1 << bit), "rep")


def params(mib):
    return pltpu.CompilerParams(vmem_limit_bytes=mib * MIB)


def cost(flops, bytes_accessed):
    return pl.CostEstimate(flops=flops // 1024, bytes_accessed=bytes_accessed // 1024, transcendentals=0)


def combine_kernel(*refs, outs):
    refs[-1][...] = jnp.zeros((8, 128), F32)
    for out, segments in zip(refs[-len(outs) - 1 : -1], outs, strict=True):
        at = 0
        for terms in segments:
            rows = terms[0][2]
            if len(terms) == 1:
                (source, start, _), = terms
                out[at : at + rows, :] = refs[source][start : start + rows, :]
            else:
                total = None
                for source, start, _ in terms:
                    part = refs[source][start : start + rows, :].astype(F32)
                    total = part if total is None else total + part
                out[at : at + rows, :] = total.astype(BF)
            at += rows


def combine(inputs, outs, after=()):
    specs, args = [], []
    for given in inputs:
        array, rows, index = given if isinstance(given, tuple) else (given, given.shape[0], 0)
        specs.append(pl.BlockSpec((rows, array.shape[1]), lambda i, index=index: (index, 0)))
        args.append(array)
    width = args[0].shape[1]
    specs += [TOKEN] * len(after)
    args += list(after)
    sizes = [sum(terms[0][2] for terms in segments) for segments in outs]
    shapes = [jax.ShapeDtypeStruct((rows, width), BF) for rows in sizes]
    return pl.pallas_call(
        partial(combine_kernel, outs=outs),
        grid=(1,),
        in_specs=specs,
        out_specs=[pl.BlockSpec(shape.shape, lambda i: (0, 0)) for shape in shapes] + [TOKEN],
        out_shape=shapes + [TOKEN_SHAPE],
        compiler_params=params(16),
        cost_estimate=cost(0, 4 * width * sum(sizes)),
    )(*args)


def choose_kernel(where, *refs):
    *found, out, token = refs
    token[...] = jnp.zeros((8, 128), F32)
    for bit, given in enumerate(found):

        @pl.when(where[PICK] == bit)
        def _(given=given):
            out[...] = given[...]


def choose(where, found):
    whole = pl.BlockSpec((SHARD, KV), lambda i, p: (0, 0))
    return pl.pallas_call(
        choose_kernel,
        grid_spec=pltpu.PrefetchScalarGridSpec(
            num_scalar_prefetch=1,
            grid=(1,),
            in_specs=[whole] * len(found),
            out_specs=[whole, TOKEN],
        ),
        out_shape=[jax.ShapeDtypeStruct((SHARD, KV), BF), TOKEN_SHAPE],
        compiler_params=params(8),
        cost_estimate=cost(0, MIB),
    )(where, *found)


def prep_kernel(where, rate, acts, mine, give):
    y, core = where[Y], where[CORE]
    for k in range(2):
        y_at = lax.rem(y + k, 2)
        to = slice(k * SHARD, (k + 1) * SHARD)
        own = pl.multiple_of((y_at * 2 + core) * SHARD, SHARD)
        sib = pl.multiple_of((y_at * 2 + 1 - core) * SHARD, SHARD)
        mine[:, to] = acts[:, pl.ds(own, SHARD)]
        give[:, to] = acts[:, pl.ds(sib, SHARD)]


def prep(where, rate, acts):
    half = jax.ShapeDtypeStruct((SHARD, 4096), BF)
    return pl.pallas_call(
        prep_kernel,
        grid_spec=pltpu.PrefetchScalarGridSpec(
            num_scalar_prefetch=2,
            grid=(Z,),
            in_specs=[pl.BlockSpec((SHARD, 1024), lambda i, w, _: (0, w[i]))],
            out_specs=[pl.BlockSpec((SHARD, 512), lambda i, *_: (0, i))] * 2,
        ),
        out_shape=[half, half],
        compiler_params=params(8),
        cost_estimate=cost(0, 8 * MIB),
    )(where, rate, acts)


def partials_kernel(mine, got, cot, got_cot, first, second, third, local, token, turned, *, scale):
    step = pl.program_id(0)
    token[...] = jnp.zeros((8, 128), F32)

    @pl.when(step == 0)
    def _():
        turned[:, :SHARD] = cot[...].T
        turned[:, SHARD:] = got_cot[...].T

    total = jnp.dot(turned[:, :SHARD], mine[...], preferred_element_type=F32)
    total += jnp.dot(turned[:, SHARD:], got[...], preferred_element_type=F32)
    total = (total * scale).astype(BF)
    own_a, own_b, other_a, other_b = (total[:, k * HALF : (k + 1) * HALF] for k in range(4))
    local[0:KV, :] = own_a
    local[KV : 2 * KV, :] = own_b
    local[2 * KV :, :] = other_b

    @pl.when(step == 0)
    def _():
        first[0:KV, :] = other_a
        first[KV : 2 * KV, :] = other_b

    for i in range(1, Z):

        @pl.when(step == i)
        def _(i=i):
            out, at = (second, i - 1) if i < 3 else (third, i - 3)
            out[at * KV : (at + 1) * KV, :] = other_a


def partials(mine, got, cot, got_cot, scale):
    columns = pl.BlockSpec((SHARD, 512), lambda i: (0, i))
    held = pl.BlockSpec((SHARD, KV), lambda i: (0, 0))
    sizes = (2 * KV, 2 * KV, 5 * KV)
    return pl.pallas_call(
        partial(partials_kernel, scale=scale),
        grid=(Z,),
        in_specs=[columns, columns, held, held],
        out_specs=[pl.BlockSpec((rows, HALF), lambda i: (0, 0)) for rows in sizes]
        + [pl.BlockSpec((3 * KV, HALF), lambda i: (i, 0)), TOKEN],
        out_shape=[jax.ShapeDtypeStruct((rows, HALF), BF) for rows in sizes + (Z * 3 * KV,)] + [TOKEN_SHAPE],
        scratch_shapes=[pltpu.VMEM((KV, 512), BF)],
        compiler_params=params(16),
        cost_estimate=cost(2 * 4096 * 512 * 512, 9 * MIB),
    )(mine, got, cot, got_cot)


def products_kernel(*refs, plan, n_pieces, first, last, scale):
    pieces = refs[:n_pieces]
    mine, got, cot, got_cot, _, *rest = refs[n_pieces:]
    if not first:
        total_in, *rest = rest
    step = pl.program_id(0)
    block = rest[-1]
    rest[-2][...] = jnp.zeros((8, 128), F32)
    for i, entry in enumerate(plan):

        @pl.when(step == i)
        def _(entry=entry):
            at = 0
            for piece, start, rows in entry:
                block[at : at + rows, :] = pieces[piece][start : start + rows, :]
                at += rows

    across = (((1,), (1,)), ((), ()))
    here = (lax.dot_general(cot[...], block[...], across, preferred_element_type=F32) * scale).astype(BF)
    there = (lax.dot_general(got_cot[...], block[...], across, preferred_element_type=F32) * scale).astype(BF)
    own = jnp.dot(mine[...], block[...], preferred_element_type=F32)
    sib = jnp.dot(got[...], block[...], preferred_element_type=F32)
    if last:
        in_here, total, tail, token, _ = rest
        in_here[...] = here
        tail[:, :512] = there
        total[...] = total_in[:SHARD, :] + own
        tail[:, 512:] = (total_in[SHARD:, :] + sib).astype(BF)
        return
    in_here, in_there, total, token, _ = rest
    in_here[...] = here
    in_there[...] = there

    @pl.when(step == 0)
    def _():
        if first:
            total[:SHARD, :] = own
            total[SHARD:, :] = sib
        else:
            total[:SHARD, :] = total_in[:SHARD, :] + own
            total[SHARD:, :] = total_in[SHARD:, :] + sib

    @pl.when(step > 0)
    def _():
        total[:SHARD, :] += own
        total[SHARD:, :] += sib


def products(base, plan, pieces, mine, got, cot, got_cot, total, scale, after, last=False):
    n = len(plan)
    whole = lambda a: pl.BlockSpec(a.shape, lambda i: (0, 0))
    columns = pl.BlockSpec((SHARD, 512), lambda i: (0, base + i))
    out_columns = pl.BlockSpec((SHARD, 512), lambda i: (0, i))
    args = list(pieces) + [mine, got, cot, got_cot, after]
    in_specs = [whole(p) for p in pieces] + [columns, columns, whole(cot), whole(cot), TOKEN]
    if total is not None:
        args.append(total)
        in_specs.append(whole(total))
    wide = jax.ShapeDtypeStruct((SHARD, 512 * n), BF)
    if last:
        shapes = [wide, jax.ShapeDtypeStruct((SHARD, KV), F32), jax.ShapeDtypeStruct((SHARD, 1024), BF)]
        out_specs = [out_columns, whole(shapes[1]), whole(shapes[2]), TOKEN]
    else:
        shapes = [wide, wide, jax.ShapeDtypeStruct((512, KV), F32)]
        out_specs = [out_columns, out_columns, whole(shapes[2]), TOKEN]
    return pl.pallas_call(
        partial(products_kernel, plan=plan, n_pieces=len(pieces), first=total is None, last=last, scale=scale),
        grid=(n,),
        in_specs=in_specs,
        out_specs=out_specs,
        out_shape=shapes + [TOKEN_SHAPE],
        scratch_shapes=[pltpu.VMEM((512, KV), BF)],
        compiler_params=params(20),
        cost_estimate=cost(n * 8 * SHARD * 512 * 512, (n + 4) * MIB),
    )(*args)


def place_kernel(where, own, sib, *rest):
    out = rest[-1]
    y, core = where[Y], where[CORE]
    for k in range(2):
        y_at = lax.rem(y + k, 2)
        part = slice(k * SHARD, (k + 1) * SHARD)
        out[:, pl.ds(pl.multiple_of((y_at * 2 + core) * SHARD, SHARD), SHARD)] = own[:, part]
        out[:, pl.ds(pl.multiple_of((y_at * 2 + 1 - core) * SHARD, SHARD), SHARD)] = sib[:, part]


def place_last_kernel(where, own, sib, total, _, out, values, *, scale):
    place_kernel(where, own, sib, out)
    values[...] = ((total[...] + sib[:, 512:].astype(F32)) * scale).astype(BF)


def place(where, base, own, sib, into, total=None, scale=None):
    n = own.shape[1] // 512
    columns = pl.BlockSpec((SHARD, 512), lambda i, w: (0, i))
    held = pl.BlockSpec((SHARD, KV), lambda i, w: (0, 0))
    args, specs, aliases = [own, sib], [columns, columns], {}
    out_specs = [pl.BlockSpec((SHARD, 1024), lambda i, w: (0, w[base + i]))]
    shapes = [jax.ShapeDtypeStruct((SHARD, 8192), BF)]
    kernel = place_kernel
    if total is not None:
        kernel = partial(place_last_kernel, scale=scale)
        args.append(total)
        specs = [columns, pl.BlockSpec((SHARD, 1024), lambda i, w: (0, 0)), held]
        out_specs.append(held)
        shapes.append(jax.ShapeDtypeStruct((SHARD, KV), BF))
    if into is not None:
        args.append(into)
        specs.append(pl.BlockSpec(memory_space=pl.ANY))
        aliases = {len(args): 0}
    return pl.pallas_call(
        kernel,
        grid_spec=pltpu.PrefetchScalarGridSpec(
            num_scalar_prefetch=1, grid=(n,), in_specs=specs, out_specs=out_specs
        ),
        out_shape=shapes,
        input_output_aliases=aliases,
        compiler_params=params(8),
        cost_estimate=cost(0, n * MIB),
    )(where, *args)


def moved_kernel(local, from_y, su, sd, yf, momentum, moved, short):
    def add(*parts):
        total = parts[0].astype(F32)
        for part in parts[1:]:
            total = total + part.astype(F32)
        return total.T

    low = add(local[0:KV, :], from_y[...], su[0:KV, :], sd[0:KV, :])
    high = add(local[KV : 2 * KV, :], su[KV:, :], sd[KV:, :], yf[...])
    new_low = 0.9 * momentum[0:HALF, :] + low
    new_high = 0.9 * momentum[HALF:, :] + high
    moved[0:HALF, :] = new_low
    moved[HALF:, :] = new_high
    short[0:HALF, :] = new_low.astype(BF)
    short[HALF:, :] = new_high.astype(BF)


def move(local, from_y, su, sd, yf, momentum):
    whole = lambda rows, cols, index=0: pl.BlockSpec((rows, cols), lambda i: (index, 0))
    return pl.pallas_call(
        moved_kernel,
        grid=(1,),
        in_specs=[
            whole(3 * KV, HALF, Z - 1),
            whole(KV, HALF, 4),
            whole(2 * KV, HALF),
            whole(2 * KV, HALF),
            whole(KV, HALF),
            whole(SHARD, KV),
        ],
        out_specs=[whole(SHARD, KV), whole(SHARD, KV)],
        out_shape=[jax.ShapeDtypeStruct((SHARD, KV), F32), jax.ShapeDtypeStruct((SHARD, KV), BF)],
        compiler_params=params(16),
        cost_estimate=cost(0, 3 * MIB),
    )(local, from_y, su, sd, yf, momentum)


def average_kernel(where, rate, weight, moved, other_w, found, new_w, new_m):
    def step(given, by):
        return (given.astype(F32) - rate[0] * by).astype(BF).astype(F32)

    other_m = found[0][...]
    for bit in range(1, len(found)):
        other_m = jnp.where(where[PICK] == bit, found[bit][...], other_m)
    other_m = other_m.astype(F32)
    new_m[...] = (moved[...] + other_m) * 0.5
    new_w[...] = ((step(weight[...], moved[...]) + step(other_w[...], other_m)) * 0.5).astype(BF)


def average(where, rate, weight, moved, other_w, found):
    def kernel(where, rate, weight, moved, other_w, *rest):
        average_kernel(where, rate, weight, moved, other_w, rest[:-2], *rest[-2:])

    rows = pl.BlockSpec((HALF, KV), lambda i, *_: (i, 0))
    return pl.pallas_call(
        kernel,
        grid_spec=pltpu.PrefetchScalarGridSpec(
            num_scalar_prefetch=2,
            grid=(SHARD // HALF,),
            in_specs=[rows] * (3 + len(found)),
            out_specs=[rows, rows],
        ),
        out_shape=[jax.ShapeDtypeStruct((SHARD, KV), BF), jax.ShapeDtypeStruct((SHARD, KV), F32)],
        compiler_params=params(8),
        cost_estimate=cost(0, 3 * MIB),
    )(where, rate, weight, moved, other_w, *found)


def per_device(activations, weights, momentum, cotangent, step_index):
    acts, cot, w = activations[0], cotangent[0], weights[0]
    scale = 1.0 / (8192.0**0.5)
    me = lax.axis_index("fsdp")
    z, y, core = me // 4, (me // 2) % 2, me % 2

    bits = lax.axis_size("rep").bit_length() - 1
    step_float = step_index.astype(F32)
    rate = 0.1 * (0.5 + 0.5 * jnp.cos(jnp.float32(3.141592653589793) * step_float / 1000.0))
    where = jnp.stack([(z + d + Z) % Z for d in ORDER] + [y, core, step_index[0] % bits]).astype(jnp.int32)

    found = [from_partner(w, bit=bit) for bit in range(bits)]
    other_w, t_w = choose(where, found)

    u1, d1, y0 = up(w), down(w), y_swap(w)

    mine, give = prep(where, rate, acts)
    got, got_cot = core_swap(give), core_swap(cot)

    to_y0, to_y1, to_y2, local, t_part = partials(mine, got, cot, got_cot, scale)

    pay_u, pay_d, pay_y, _ = combine(
        [u1, d1, y0],
        [
            [[(0, HALF, HALF)], [(0, 0, HALF)], [(2, HALF, HALF)]],
            [[(1, 0, SHARD)], [(2, HALF, HALF)]],
            [[(0, 0, HALF)], [(1, 0, HALF)]],
        ]
    )
    u2, d2, y1 = up(pay_u), down(pay_d), y_swap(pay_y)
    from_y0, from_y1, from_y2 = y_swap(to_y0), y_swap(to_y1), y_swap(to_y2)

    def loc(i):
        return (local, 3 * KV, i)

    own, own_high, other = 0, KV, 2 * KV
    pay_u, pay_d, t_s1 = combine(
        [loc(0), loc(1), loc(2), from_y0],
        [
            [[(0, own, KV), (3, 0, KV)], [(1, other, KV)]],
            [[(0, own_high, KV), (3, KV, KV)], [(2, other, KV)]],
        ],
    )
    su1, sd1 = up(pay_u), down(pay_d)

    pay_y, _ = combine([u2, d2], [[[(0, HALF, HALF)], [(1, 0, HALF)]]])
    u3, d3, y2 = up(u2), down(d2), y_swap(pay_y)

    total = None
    ing1, give1, total, t_g1 = products(
        5,
        (
            ((1, 0, SHARD), (3, HALF, HALF), (5, 2 * HALF, HALF)),
            ((0, 0, SHARD), (3, 0, HALF), (4, 2 * HALF, HALF)),
            ((6, 0, SHARD), (2, 0, SHARD)),
        ),
        (u1, d1, y0, y1, u2, d2, w),
        mine, got, cot, got_cot, None, scale, t_part,
    )
    got1 = core_swap(give1)

    pay_u, pay_d, t_s2 = combine(
        [loc(1), loc(2), loc(3), loc(4), (from_y1, KV, 0), (from_y1, KV, 1), su1, sd1],
        [
            [[(0, own, KV), (4, 0, KV), (6, 0, KV)], [(0, own_high, KV)], [(2, other, KV), (6, KV, KV)]],
            [[(1, own, KV), (5, 0, KV)], [(1, own_high, KV), (7, 0, KV)], [(3, other, KV), (7, KV, KV)]],
        ],
    )
    su2, sd2 = up(pay_u), down(pay_d)

    pay_u, pay_d, pay_y, _ = combine(
        [u3, d3],
        [[[(0, HALF, SHARD)]], [[(1, HALF, SHARD)]], [[(0, HALF, HALF)], [(1, 0, HALF)]]]
    )
    u4, d4, y3 = up(pay_u), down(pay_d), y_swap(pay_y)
    ing2, give2, total, t_g2 = products(
        3,
        (
            ((1, 0, SHARD), (2, HALF, HALF), (4, SHARD, HALF)),
            ((0, HALF, HALF), (0, 0, HALF), (2, 0, HALF), (3, SHARD, HALF)),
        ),
        (u2, d2, y2, u3, d3),
        mine, got, cot, got_cot, total, scale, t_part,
    )
    got2 = core_swap(give2)

    def third(own_at, y_at, other_at, got_at):
        return [
            [(own_at, own, KV), (y_at, 0, KV), (got_at, 0, KV)],
            [(own_at, own_high, KV), (got_at, KV, KV)],
            [(other_at, other, KV), (got_at, 2 * KV, KV)],
        ]

    pay_u, pay_d, t_s3 = combine(
        [loc(3), loc(4), loc(5), loc(6), (from_y2, KV, 0), (from_y2, KV, 1), su2, sd2],
        [third(0, 4, 2, 6), third(1, 5, 3, 7)]
    )
    su3, sd3 = up(pay_u), down(pay_d)

    pay_u, pay_d, pay_y, t_s4 = combine(
        [loc(5), loc(6), loc(7), (from_y2, KV, 2), (from_y2, KV, 3), su3, sd3],
        [
            [[(0, own, KV), (3, 0, KV), (5, 0, KV)], [(0, own_high, KV), (5, KV, KV)]],
            [[(1, own, KV), (4, 0, KV), (6, 0, KV)], [(1, own_high, KV), (6, KV, KV)]],
            [[(2, other, KV), (5, 2 * KV, KV), (6, 2 * KV, KV)]],
        ]
    )
    su4, sd4, yf = up(pay_u), down(pay_d), y_swap(pay_y)

    pay_y, _ = combine([u4, d4], [[[(0, 0, HALF)], [(1, 0, HALF)]]])
    y4 = y_swap(pay_y)
    ing3, give3, total, t_g3 = products(
        1,
        (
            ((1, 0, SHARD), (2, HALF, HALF), (4, HALF, HALF)),
            ((0, HALF, HALF), (0, 0, HALF), (2, 0, HALF), (3, HALF, HALF)),
        ),
        (u3, d3, y3, u4, d4),
        mine, got, cot, got_cot, total, scale, t_part,
    )
    got3 = core_swap(give3)

    ing4, total, tail, _ = products(
        0,
        (((0, 0, HALF), (1, 0, HALF), (2, 0, SHARD)),),
        (u4, d4, y4),
        mine, got, cot, got_cot, total, scale, t_part, last=True,
    )
    got4 = core_swap(tail)

    moved, short = move(local, from_y2, su4, sd4, yf, momentum[0])
    found = [from_partner(short, bit=bit) for bit in range(bits)]
    new_w, new_m = average(where, rate, w, moved, other_w, found)

    (ingrad,) = place(where, 5, ing1, got1, None)
    (ingrad,) = place(where, 3, ing2, got2, ingrad)
    (ingrad,) = place(where, 1, ing3, got3, ingrad)
    ingrad, values = place(where, 0, ing4, got4, ingrad, total, scale)
    return (values[None], ingrad[None], new_w[None], new_m[None])


def solution(mesh):
    rows = P("rep", "fsdp", None)
    return jax.shard_map(
        per_device,
        mesh=mesh,
        in_specs=(rows, rows, rows, rows, P()),
        out_specs=(rows, rows, rows, rows),
        check_vma=False,
    )
```

```python
from functools import partial

import jax
import jax.numpy as jnp
from jax import lax
from jax.experimental import pallas as pl
from jax.experimental.pallas import tpu as pltpu
from jax.sharding import PartitionSpec as P

BF = jnp.bfloat16
F32 = jnp.float32
Z = 8
HALF = 128
SHARD = 256
KV = 512
ORDER = (4, 3, -3, 2, -2, 1, -1, 0)
MIB = 2**20
Y, CORE, PICK = 8, 9, 10
TOKEN = pl.BlockSpec((8, 128), lambda *_: (0, 0))
TOKEN_SHAPE = jax.ShapeDtypeStruct((8, 128), F32)


def send(value, move, axis="fsdp"):
    pairs = [(source, move(source)) for source in range(lax.axis_size(axis))]
    return lax.ppermute(value, axis, pairs)


def up(value):
    return send(value, lambda f: (f + 4) % 32)


def down(value):
    return send(value, lambda f: (f - 4) % 32)


def y_swap(value):
    return send(value, lambda f: f ^ 2)


def core_swap(value):
    return send(value, lambda f: f ^ 1)


def from_partner(value, *, bit):
    return send(value, lambda r: r ^ (1 << bit), "rep")


def params(mib):
    return pltpu.CompilerParams(vmem_limit_bytes=mib * MIB)


def cost(flops, bytes_accessed):
    return pl.CostEstimate(flops=flops // 1024, bytes_accessed=bytes_accessed // 1024, transcendentals=0)


def combine_kernel(*refs, outs):
    refs[-1][...] = jnp.zeros((8, 128), F32)
    for out, segments in zip(refs[-len(outs) - 1 : -1], outs, strict=True):
        at = 0
        for terms in segments:
            rows = terms[0][2]
            if len(terms) == 1:
                (source, start, _), = terms
                out[at : at + rows, :] = refs[source][start : start + rows, :]
            else:
                total = None
                for source, start, _ in terms:
                    part = refs[source][start : start + rows, :].astype(F32)
                    total = part if total is None else total + part
                out[at : at + rows, :] = total.astype(BF)
            at += rows


def combine(inputs, outs, after=()):
    specs, args = [], []
    for given in inputs:
        array, rows, index = given if isinstance(given, tuple) else (given, given.shape[0], 0)
        specs.append(pl.BlockSpec((rows, array.shape[1]), lambda i, index=index: (index, 0)))
        args.append(array)
    width = args[0].shape[1]
    specs += [TOKEN if t.dtype == F32 else pl.BlockSpec((16, 128), lambda i: (0, 0)) for t in after]
    args += list(after)
    sizes = [sum(terms[0][2] for terms in segments) for segments in outs]
    shapes = [jax.ShapeDtypeStruct((rows, width), BF) for rows in sizes]
    return pl.pallas_call(
        partial(combine_kernel, outs=outs),
        grid=(1,),
        in_specs=specs,
        out_specs=[pl.BlockSpec(shape.shape, lambda i: (0, 0)) for shape in shapes] + [TOKEN],
        out_shape=shapes + [TOKEN_SHAPE],
        compiler_params=params(16),
        cost_estimate=cost(0, 4 * width * sum(sizes)),
    )(*args)


def choose_kernel(where, *refs):
    *found, out, token = refs
    token[...] = jnp.zeros((8, 128), F32)
    for bit, given in enumerate(found):

        @pl.when(where[PICK] == bit)
        def _(given=given):
            out[...] = given[...]


def choose(where, found):
    whole = pl.BlockSpec((SHARD, KV), lambda i, p: (0, 0))
    return pl.pallas_call(
        choose_kernel,
        grid_spec=pltpu.PrefetchScalarGridSpec(
            num_scalar_prefetch=1,
            grid=(1,),
            in_specs=[whole] * len(found),
            out_specs=[whole, TOKEN],
        ),
        out_shape=[jax.ShapeDtypeStruct((SHARD, KV), BF), TOKEN_SHAPE],
        compiler_params=params(8),
        cost_estimate=cost(0, MIB),
    )(where, *found)


def prep_kernel(where, rate, acts, mine, give):
    y, core = where[Y], where[CORE]
    for k in range(2):
        y_at = lax.rem(y + k, 2)
        to = slice(k * SHARD, (k + 1) * SHARD)
        own = pl.multiple_of((y_at * 2 + core) * SHARD, SHARD)
        sib = pl.multiple_of((y_at * 2 + 1 - core) * SHARD, SHARD)
        mine[:, to] = acts[:, pl.ds(own, SHARD)]
        give[:, to] = acts[:, pl.ds(sib, SHARD)]


def prep(where, rate, acts):
    half = jax.ShapeDtypeStruct((SHARD, 4096), BF)
    return pl.pallas_call(
        prep_kernel,
        grid_spec=pltpu.PrefetchScalarGridSpec(
            num_scalar_prefetch=2,
            grid=(Z,),
            in_specs=[pl.BlockSpec((SHARD, 1024), lambda i, w, _: (0, w[i]))],
            out_specs=[pl.BlockSpec((SHARD, 512), lambda i, *_: (0, i))] * 2,
        ),
        out_shape=[half, half],
        compiler_params=params(8),
        cost_estimate=cost(0, 8 * MIB),
    )(where, rate, acts)


def partials_kernel(mine, got, cot, got_cot, first, second, third, local, token, turned, *, scale):
    step = pl.program_id(0)
    token[...] = jnp.zeros((8, 128), F32)

    @pl.when(step == 0)
    def _():
        turned[:, :SHARD] = cot[...].T
        turned[:, SHARD:] = got_cot[...].T

    total = jnp.dot(turned[:, :SHARD], mine[...], preferred_element_type=F32)
    total += jnp.dot(turned[:, SHARD:], got[...], preferred_element_type=F32)
    total = (total * scale).astype(BF)
    own_a, own_b, other_a, other_b = (total[:, k * HALF : (k + 1) * HALF] for k in range(4))
    local[0:KV, :] = own_a
    local[KV : 2 * KV, :] = own_b
    local[2 * KV :, :] = other_b

    @pl.when(step == 0)
    def _():
        first[0:KV, :] = other_a
        first[KV : 2 * KV, :] = other_b

    for i in range(1, Z):

        @pl.when(step == i)
        def _(i=i):
            out, at = (second, i - 1) if i < 3 else (third, i - 3)
            out[at * KV : (at + 1) * KV, :] = other_a


def partials(mine, got, cot, got_cot, scale):
    columns = pl.BlockSpec((SHARD, 512), lambda i: (0, i))
    held = pl.BlockSpec((SHARD, KV), lambda i: (0, 0))
    sizes = (2 * KV, 2 * KV, 5 * KV)
    return pl.pallas_call(
        partial(partials_kernel, scale=scale),
        grid=(Z,),
        in_specs=[columns, columns, held, held],
        out_specs=[pl.BlockSpec((rows, HALF), lambda i: (0, 0)) for rows in sizes]
        + [pl.BlockSpec((3 * KV, HALF), lambda i: (i, 0)), TOKEN],
        out_shape=[jax.ShapeDtypeStruct((rows, HALF), BF) for rows in sizes + (Z * 3 * KV,)] + [TOKEN_SHAPE],
        scratch_shapes=[pltpu.VMEM((KV, 512), BF)],
        compiler_params=params(16),
        cost_estimate=cost(2 * 4096 * 512 * 512, 9 * MIB),
    )(mine, got, cot, got_cot)


def products_kernel(*refs, plan, n_pieces, first, last, scale):
    pieces = refs[:n_pieces]
    mine, got, cot, got_cot, _, *rest = refs[n_pieces:]
    if not first:
        total_in, *rest = rest
    step = pl.program_id(0)
    block = rest[-1]
    rest[-2][...] = jnp.zeros((8, 128), F32)
    for i, entry in enumerate(plan):

        @pl.when(step == i)
        def _(entry=entry):
            at = 0
            for piece, start, rows in entry:
                block[at : at + rows, :] = pieces[piece][start : start + rows, :]
                at += rows

    across = (((1,), (1,)), ((), ()))
    here = (lax.dot_general(cot[...], block[...], across, preferred_element_type=F32) * scale).astype(BF)
    there = (lax.dot_general(got_cot[...], block[...], across, preferred_element_type=F32) * scale).astype(BF)
    own = jnp.dot(mine[...], block[...], preferred_element_type=F32)
    sib = jnp.dot(got[...], block[...], preferred_element_type=F32)
    if last:
        in_here, total, tail, token, _ = rest
        in_here[...] = here
        tail[:, :512] = there
        total[...] = total_in[:SHARD, :] + own
        tail[:, 512:] = (total_in[SHARD:, :] + sib).astype(BF)
        return
    in_here, in_there, total, token, _ = rest
    in_here[...] = here
    in_there[...] = there

    @pl.when(step == 0)
    def _():
        if first:
            total[:SHARD, :] = own
            total[SHARD:, :] = sib
        else:
            total[:SHARD, :] = total_in[:SHARD, :] + own
            total[SHARD:, :] = total_in[SHARD:, :] + sib

    @pl.when(step > 0)
    def _():
        total[:SHARD, :] += own
        total[SHARD:, :] += sib


def products(base, plan, pieces, mine, got, cot, got_cot, total, scale, after, last=False):
    n = len(plan)
    whole = lambda a: pl.BlockSpec(a.shape, lambda i: (0, 0))
    columns = pl.BlockSpec((SHARD, 512), lambda i: (0, base + i))
    out_columns = pl.BlockSpec((SHARD, 512), lambda i: (0, i))
    args = list(pieces) + [mine, got, cot, got_cot, after]
    in_specs = [whole(p) for p in pieces] + [columns, columns, whole(cot), whole(cot), TOKEN]
    if total is not None:
        args.append(total)
        in_specs.append(whole(total))
    wide = jax.ShapeDtypeStruct((SHARD, 512 * n), BF)
    if last:
        shapes = [wide, jax.ShapeDtypeStruct((SHARD, KV), F32), jax.ShapeDtypeStruct((SHARD, 1024), BF)]
        out_specs = [out_columns, whole(shapes[1]), whole(shapes[2]), TOKEN]
    else:
        shapes = [wide, wide, jax.ShapeDtypeStruct((512, KV), F32)]
        out_specs = [out_columns, out_columns, whole(shapes[2]), TOKEN]
    return pl.pallas_call(
        partial(products_kernel, plan=plan, n_pieces=len(pieces), first=total is None, last=last, scale=scale),
        grid=(n,),
        in_specs=in_specs,
        out_specs=out_specs,
        out_shape=shapes + [TOKEN_SHAPE],
        scratch_shapes=[pltpu.VMEM((512, KV), BF)],
        compiler_params=params(20),
        cost_estimate=cost(n * 8 * SHARD * 512 * 512, (n + 4) * MIB),
    )(*args)


def place_kernel(where, own, sib, *rest):
    out = rest[-1]
    y, core = where[Y], where[CORE]
    for k in range(2):
        y_at = lax.rem(y + k, 2)
        part = slice(k * SHARD, (k + 1) * SHARD)
        out[:, pl.ds(pl.multiple_of((y_at * 2 + core) * SHARD, SHARD), SHARD)] = own[:, part]
        out[:, pl.ds(pl.multiple_of((y_at * 2 + 1 - core) * SHARD, SHARD), SHARD)] = sib[:, part]


def place_last_kernel(where, own, sib, total, _, out, values, *, scale):
    place_kernel(where, own, sib, out)
    values[...] = ((total[...] + sib[:, 512:].astype(F32)) * scale).astype(BF)


def place(where, base, own, sib, into, total=None, scale=None):
    n = own.shape[1] // 512
    columns = pl.BlockSpec((SHARD, 512), lambda i, w: (0, i))
    held = pl.BlockSpec((SHARD, KV), lambda i, w: (0, 0))
    args, specs, aliases = [own, sib], [columns, columns], {}
    out_specs = [pl.BlockSpec((SHARD, 1024), lambda i, w: (0, w[base + i]))]
    shapes = [jax.ShapeDtypeStruct((SHARD, 8192), BF)]
    kernel = place_kernel
    if total is not None:
        kernel = partial(place_last_kernel, scale=scale)
        args.append(total)
        specs = [columns, pl.BlockSpec((SHARD, 1024), lambda i, w: (0, 0)), held]
        out_specs.append(held)
        shapes.append(jax.ShapeDtypeStruct((SHARD, KV), BF))
    if into is not None:
        args.append(into)
        specs.append(pl.BlockSpec(memory_space=pl.ANY))
        aliases = {len(args): 0}
    return pl.pallas_call(
        kernel,
        grid_spec=pltpu.PrefetchScalarGridSpec(
            num_scalar_prefetch=1, grid=(n,), in_specs=specs, out_specs=out_specs
        ),
        out_shape=shapes,
        input_output_aliases=aliases,
        compiler_params=params(8),
        cost_estimate=cost(0, n * MIB),
    )(where, *args)


def moved_kernel(local, from_y, su, sd, yf, momentum, moved, short):
    def add(*parts):
        total = parts[0].astype(F32)
        for part in parts[1:]:
            total = total + part.astype(F32)
        return total.T

    low = add(local[0:KV, :], from_y[...], su[0:KV, :], sd[0:KV, :])
    high = add(local[KV : 2 * KV, :], su[KV:, :], sd[KV:, :], yf[...])
    new_low = 0.9 * momentum[0:HALF, :] + low
    new_high = 0.9 * momentum[HALF:, :] + high
    moved[0:HALF, :] = new_low
    moved[HALF:, :] = new_high
    short[0:HALF, :] = new_low.astype(BF)
    short[HALF:, :] = new_high.astype(BF)


def move(local, from_y, su, sd, yf, momentum):
    whole = lambda rows, cols, index=0: pl.BlockSpec((rows, cols), lambda i: (index, 0))
    return pl.pallas_call(
        moved_kernel,
        grid=(1,),
        in_specs=[
            whole(3 * KV, HALF, Z - 1),
            whole(KV, HALF, 4),
            whole(2 * KV, HALF),
            whole(2 * KV, HALF),
            whole(KV, HALF),
            whole(SHARD, KV),
        ],
        out_specs=[whole(SHARD, KV), whole(SHARD, KV)],
        out_shape=[jax.ShapeDtypeStruct((SHARD, KV), F32), jax.ShapeDtypeStruct((SHARD, KV), BF)],
        compiler_params=params(16),
        cost_estimate=cost(0, 3 * MIB),
    )(local, from_y, su, sd, yf, momentum)


def average_kernel(where, rate, weight, moved, other_w, found, new_w, new_m):
    def step(given, by):
        return (given.astype(F32) - rate[0] * by).astype(BF).astype(F32)

    other_m = found[0][...]
    for bit in range(1, len(found)):
        other_m = jnp.where(where[PICK] == bit, found[bit][...], other_m)
    other_m = other_m.astype(F32)
    new_m[...] = (moved[...] + other_m) * 0.5
    new_w[...] = ((step(weight[...], moved[...]) + step(other_w[...], other_m)) * 0.5).astype(BF)


def average(where, rate, weight, moved, other_w, found):
    def kernel(where, rate, weight, moved, other_w, *rest):
        average_kernel(where, rate, weight, moved, other_w, rest[:-2], *rest[-2:])

    rows = pl.BlockSpec((HALF, KV), lambda i, *_: (i, 0))
    return pl.pallas_call(
        kernel,
        grid_spec=pltpu.PrefetchScalarGridSpec(
            num_scalar_prefetch=2,
            grid=(SHARD // HALF,),
            in_specs=[rows] * (3 + len(found)),
            out_specs=[rows, rows],
        ),
        out_shape=[jax.ShapeDtypeStruct((SHARD, KV), BF), jax.ShapeDtypeStruct((SHARD, KV), F32)],
        compiler_params=params(8),
        cost_estimate=cost(0, 3 * MIB),
    )(where, rate, weight, moved, other_w, *found)


def per_device(activations, weights, momentum, cotangent, step_index):
    acts, cot, w = activations[0], cotangent[0], weights[0]
    scale = 1.0 / (8192.0**0.5)
    me = lax.axis_index("fsdp")
    z, y, core = me // 4, (me // 2) % 2, me % 2

    bits = lax.axis_size("rep").bit_length() - 1
    step_float = step_index.astype(F32)
    rate = 0.1 * (0.5 + 0.5 * jnp.cos(jnp.float32(3.141592653589793) * step_float / 1000.0))
    where = jnp.stack([(z + d + Z) % Z for d in ORDER] + [y, core, step_index[0] % bits]).astype(jnp.int32)

    found = [from_partner(w, bit=bit) for bit in range(bits)]
    other_w, t_w = choose(where, found)

    u1, d1, y0 = up(w), down(w), y_swap(w)

    mine, give = prep(where, rate, acts)
    got, got_cot = core_swap(give), core_swap(cot)

    to_y0, to_y1, to_y2, local, t_part = partials(mine, got, cot, got_cot, scale)

    pay_u, pay_d, pay_y, _ = combine(
        [u1, d1, y0],
        [
            [[(0, HALF, HALF)], [(0, 0, HALF)], [(2, HALF, HALF)]],
            [[(1, 0, SHARD)], [(2, HALF, HALF)]],
            [[(0, 0, HALF)], [(1, 0, HALF)]],
        ]
    )
    u2, d2, y1 = up(pay_u), down(pay_d), y_swap(pay_y)
    from_y0, from_y1, from_y2 = y_swap(to_y0), y_swap(to_y1), y_swap(to_y2)

    def loc(i):
        return (local, 3 * KV, i)

    own, own_high, other = 0, KV, 2 * KV
    pay_u, pay_d, t_s1 = combine(
        [loc(0), loc(1), loc(2), from_y0],
        [
            [[(0, own, KV), (3, 0, KV)], [(1, other, KV)]],
            [[(0, own_high, KV), (3, KV, KV)], [(2, other, KV)]],
        ],
    )
    su1, sd1 = up(pay_u), down(pay_d)

    pay_y, _ = combine([u2, d2], [[[(0, HALF, HALF)], [(1, 0, HALF)]]])
    u3, d3, y2 = up(u2), down(d2), y_swap(pay_y)

    total = None
    ing1, give1, total, t_g1 = products(
        5,
        (
            ((1, 0, SHARD), (3, HALF, HALF), (5, 2 * HALF, HALF)),
            ((0, 0, SHARD), (3, 0, HALF), (4, 2 * HALF, HALF)),
            ((6, 0, SHARD), (2, 0, SHARD)),
        ),
        (u1, d1, y0, y1, u2, d2, w),
        mine, got, cot, got_cot, None, scale, t_part,
    )
    got1 = core_swap(give1)

    pay_u, pay_d, t_s2 = combine(
        [loc(1), loc(2), loc(3), loc(4), (from_y1, KV, 0), (from_y1, KV, 1), su1, sd1],
        [
            [[(0, own, KV), (4, 0, KV), (6, 0, KV)], [(0, own_high, KV)], [(2, other, KV), (6, KV, KV)]],
            [[(1, own, KV), (5, 0, KV)], [(1, own_high, KV), (7, 0, KV)], [(3, other, KV), (7, KV, KV)]],
        ],
    )
    su2, sd2 = up(pay_u), down(pay_d)

    pay_u, pay_d, pay_y, _ = combine(
        [u3, d3],
        [[[(0, HALF, SHARD)]], [[(1, HALF, SHARD)]], [[(0, HALF, HALF)], [(1, 0, HALF)]]]
    )
    u4, d4, y3 = up(pay_u), down(pay_d), y_swap(pay_y)
    ing2, give2, total, t_g2 = products(
        3,
        (
            ((1, 0, SHARD), (2, HALF, HALF), (4, SHARD, HALF)),
            ((0, HALF, HALF), (0, 0, HALF), (2, 0, HALF), (3, SHARD, HALF)),
        ),
        (u2, d2, y2, u3, d3),
        mine, got, cot, got_cot, total, scale, t_part,
    )
    got2 = core_swap(give2)

    def third(own_at, y_at, other_at, got_at):
        return [
            [(own_at, own, KV), (y_at, 0, KV), (got_at, 0, KV)],
            [(own_at, own_high, KV), (got_at, KV, KV)],
            [(other_at, other, KV), (got_at, 2 * KV, KV)],
        ]

    pay_u, pay_d, t_s3 = combine(
        [loc(3), loc(4), loc(5), loc(6), (from_y2, KV, 0), (from_y2, KV, 1), su2, sd2],
        [third(0, 4, 2, 6), third(1, 5, 3, 7)],
        after=(t_w,),
    )
    su3, sd3 = up(pay_u), down(pay_d)

    pay_u, pay_d, pay_y, t_s4 = combine(
        [loc(5), loc(6), loc(7), (from_y2, KV, 2), (from_y2, KV, 3), su3, sd3],
        [
            [[(0, own, KV), (3, 0, KV), (5, 0, KV)], [(0, own_high, KV), (5, KV, KV)]],
            [[(1, own, KV), (4, 0, KV), (6, 0, KV)], [(1, own_high, KV), (6, KV, KV)]],
            [[(2, other, KV), (5, 2 * KV, KV), (6, 2 * KV, KV)]],
        ]
    )
    su4, sd4, yf = up(pay_u), down(pay_d), y_swap(pay_y)

    pay_y, _ = combine([u4, d4], [[[(0, 0, HALF)], [(1, 0, HALF)]]])
    y4 = y_swap(pay_y)
    ing3, give3, total, t_g3 = products(
        1,
        (
            ((1, 0, SHARD), (2, HALF, HALF), (4, HALF, HALF)),
            ((0, HALF, HALF), (0, 0, HALF), (2, 0, HALF), (3, HALF, HALF)),
        ),
        (u3, d3, y3, u4, d4),
        mine, got, cot, got_cot, total, scale, t_part,
    )
    got3 = core_swap(give3)

    ing4, total, tail, _ = products(
        0,
        (((0, 0, HALF), (1, 0, HALF), (2, 0, SHARD)),),
        (u4, d4, y4),
        mine, got, cot, got_cot, total, scale, t_part, last=True,
    )
    got4 = core_swap(tail)

    moved, short = move(local, from_y2, su4, sd4, yf, momentum[0])
    found = [from_partner(short, bit=bit) for bit in range(bits)]
    new_w, new_m = average(where, rate, w, moved, other_w, found)

    (ingrad,) = place(where, 5, ing1, got1, None)
    (ingrad,) = place(where, 3, ing2, got2, ingrad)
    (ingrad,) = place(where, 1, ing3, got3, ingrad)
    ingrad, values = place(where, 0, ing4, got4, ingrad, total, scale)
    return (values[None], ingrad[None], new_w[None], new_m[None])


def solution(mesh):
    rows = P("rep", "fsdp", None)
    return jax.shard_map(
        per_device,
        mesh=mesh,
        in_specs=(rows, rows, rows, rows, P()),
        out_specs=(rows, rows, rows, rows),
        check_vma=False,
    )
```

```python
from functools import partial

import jax
import jax.numpy as jnp
from jax import lax
from jax.experimental import pallas as pl
from jax.experimental.pallas import tpu as pltpu
from jax.sharding import PartitionSpec as P

BF = jnp.bfloat16
F32 = jnp.float32
Z = 8
HALF = 128
SHARD = 256
KV = 512
ORDER = (4, 3, -3, 2, -2, 1, -1, 0)
MIB = 2**20
Y, CORE, PICK = 8, 9, 10
TOKEN = pl.BlockSpec((8, 128), lambda *_: (0, 0))
TOKEN_SHAPE = jax.ShapeDtypeStruct((8, 128), F32)


def send(value, move, axis="fsdp"):
    pairs = [(source, move(source)) for source in range(lax.axis_size(axis))]
    return lax.ppermute(value, axis, pairs)


def up(value):
    return send(value, lambda f: (f + 4) % 32)


def down(value):
    return send(value, lambda f: (f - 4) % 32)


def y_swap(value):
    return send(value, lambda f: f ^ 2)


def core_swap(value):
    return send(value, lambda f: f ^ 1)


def from_partner(value, *, bit):
    return send(value, lambda r: r ^ (1 << bit), "rep")


def params(mib):
    return pltpu.CompilerParams(vmem_limit_bytes=mib * MIB)


def cost(flops, bytes_accessed):
    return pl.CostEstimate(flops=flops // 1024, bytes_accessed=bytes_accessed // 1024, transcendentals=0)


def combine_kernel(*refs, outs):
    refs[-1][...] = jnp.zeros((8, 128), F32)
    for out, segments in zip(refs[-len(outs) - 1 : -1], outs, strict=True):
        at = 0
        for terms in segments:
            rows = terms[0][2]
            if len(terms) == 1:
                (source, start, _), = terms
                out[at : at + rows, :] = refs[source][start : start + rows, :]
            else:
                total = None
                for source, start, _ in terms:
                    part = refs[source][start : start + rows, :].astype(F32)
                    total = part if total is None else total + part
                out[at : at + rows, :] = total.astype(BF)
            at += rows


def combine(inputs, outs, after=()):
    specs, args = [], []
    for given in inputs:
        array, rows, index = given if isinstance(given, tuple) else (given, given.shape[0], 0)
        specs.append(pl.BlockSpec((rows, array.shape[1]), lambda i, index=index: (index, 0)))
        args.append(array)
    width = args[0].shape[1]
    specs += [TOKEN if t.dtype == F32 else pl.BlockSpec((16, 128), lambda i: (0, 0)) for t in after]
    args += list(after)
    sizes = [sum(terms[0][2] for terms in segments) for segments in outs]
    shapes = [jax.ShapeDtypeStruct((rows, width), BF) for rows in sizes]
    return pl.pallas_call(
        partial(combine_kernel, outs=outs),
        grid=(1,),
        in_specs=specs,
        out_specs=[pl.BlockSpec(shape.shape, lambda i: (0, 0)) for shape in shapes] + [TOKEN],
        out_shape=shapes + [TOKEN_SHAPE],
        compiler_params=params(16),
        cost_estimate=cost(0, 4 * width * sum(sizes)),
    )(*args)


def choose_kernel(where, *refs):
    *found, out, token = refs
    token[...] = jnp.zeros((8, 128), F32)
    for bit, given in enumerate(found):

        @pl.when(where[PICK] == bit)
        def _(given=given):
            out[...] = given[...]


def choose(where, found):
    whole = pl.BlockSpec((SHARD, KV), lambda i, p: (0, 0))
    return pl.pallas_call(
        choose_kernel,
        grid_spec=pltpu.PrefetchScalarGridSpec(
            num_scalar_prefetch=1,
            grid=(1,),
            in_specs=[whole] * len(found),
            out_specs=[whole, TOKEN],
        ),
        out_shape=[jax.ShapeDtypeStruct((SHARD, KV), BF), TOKEN_SHAPE],
        compiler_params=params(8),
        cost_estimate=cost(0, MIB),
    )(where, *found)


def prep_kernel(where, rate, acts, mine, give):
    y, core = where[Y], where[CORE]
    for k in range(2):
        y_at = lax.rem(y + k, 2)
        to = slice(k * SHARD, (k + 1) * SHARD)
        own = pl.multiple_of((y_at * 2 + core) * SHARD, SHARD)
        sib = pl.multiple_of((y_at * 2 + 1 - core) * SHARD, SHARD)
        mine[:, to] = acts[:, pl.ds(own, SHARD)]
        give[:, to] = acts[:, pl.ds(sib, SHARD)]


def prep(where, rate, acts):
    half = jax.ShapeDtypeStruct((SHARD, 4096), BF)
    return pl.pallas_call(
        prep_kernel,
        grid_spec=pltpu.PrefetchScalarGridSpec(
            num_scalar_prefetch=2,
            grid=(Z,),
            in_specs=[pl.BlockSpec((SHARD, 1024), lambda i, w, _: (0, w[i]))],
            out_specs=[pl.BlockSpec((SHARD, 512), lambda i, *_: (0, i))] * 2,
        ),
        out_shape=[half, half],
        compiler_params=params(8),
        cost_estimate=cost(0, 8 * MIB),
    )(where, rate, acts)


def partials_kernel(mine, got, cot, got_cot, first, second, third, local, token, turned, both, *, scale):
    step = pl.program_id(0)
    token[...] = jnp.zeros((8, 128), F32)

    @pl.when(step == 0)
    def _():
        turned[:, :SHARD] = cot[...].T
        turned[:, SHARD:] = got_cot[...].T

    both[:SHARD, :] = mine[...]
    both[SHARD:, :] = got[...]
    total = jnp.dot(turned[...], both[...], preferred_element_type=F32)
    total = (total * scale).astype(BF)
    own_a, own_b, other_a, other_b = (total[:, k * HALF : (k + 1) * HALF] for k in range(4))
    local[0:KV, :] = own_a
    local[KV : 2 * KV, :] = own_b
    local[2 * KV :, :] = other_b

    @pl.when(step == 0)
    def _():
        first[0:KV, :] = other_a
        first[KV : 2 * KV, :] = other_b

    for i in range(1, Z):

        @pl.when(step == i)
        def _(i=i):
            out, at = (second, i - 1) if i < 3 else (third, i - 3)
            out[at * KV : (at + 1) * KV, :] = other_a


def partials(mine, got, cot, got_cot, scale):
    columns = pl.BlockSpec((SHARD, 512), lambda i: (0, i))
    held = pl.BlockSpec((SHARD, KV), lambda i: (0, 0))
    sizes = (2 * KV, 2 * KV, 5 * KV)
    return pl.pallas_call(
        partial(partials_kernel, scale=scale),
        grid=(Z,),
        in_specs=[columns, columns, held, held],
        out_specs=[pl.BlockSpec((rows, HALF), lambda i: (0, 0)) for rows in sizes]
        + [pl.BlockSpec((3 * KV, HALF), lambda i: (i, 0)), TOKEN],
        out_shape=[jax.ShapeDtypeStruct((rows, HALF), BF) for rows in sizes + (Z * 3 * KV,)] + [TOKEN_SHAPE],
        scratch_shapes=[pltpu.VMEM((KV, 512), BF), pltpu.VMEM((512, 512), BF)],
        compiler_params=params(16),
        cost_estimate=cost(2 * 4096 * 512 * 512, 9 * MIB),
    )(mine, got, cot, got_cot)


def products_kernel(*refs, plan, n_pieces, first, last, scale):
    pieces = refs[:n_pieces]
    mine, got, cot, got_cot, _, *rest = refs[n_pieces:]
    if not first:
        total_in, *rest = rest
    step = pl.program_id(0)
    block = rest[-1]
    rest[-2][...] = jnp.zeros((8, 128), F32)
    for i, entry in enumerate(plan):

        @pl.when(step == i)
        def _(entry=entry):
            at = 0
            for piece, start, rows in entry:
                block[at : at + rows, :] = pieces[piece][start : start + rows, :]
                at += rows

    across = (((1,), (1,)), ((), ()))
    here = (lax.dot_general(cot[...], block[...], across, preferred_element_type=F32) * scale).astype(BF)
    there = (lax.dot_general(got_cot[...], block[...], across, preferred_element_type=F32) * scale).astype(BF)
    own = jnp.dot(mine[...], block[...], preferred_element_type=F32)
    sib = jnp.dot(got[...], block[...], preferred_element_type=F32)
    if last:
        in_here, total, tail, token, _ = rest
        in_here[...] = here
        tail[:, :512] = there
        total[...] = total_in[:SHARD, :] + own
        tail[:, 512:] = (total_in[SHARD:, :] + sib).astype(BF)
        return
    in_here, in_there, total, token, _ = rest
    in_here[...] = here
    in_there[...] = there

    @pl.when(step == 0)
    def _():
        if first:
            total[:SHARD, :] = own
            total[SHARD:, :] = sib
        else:
            total[:SHARD, :] = total_in[:SHARD, :] + own
            total[SHARD:, :] = total_in[SHARD:, :] + sib

    @pl.when(step > 0)
    def _():
        total[:SHARD, :] += own
        total[SHARD:, :] += sib


def products(base, plan, pieces, mine, got, cot, got_cot, total, scale, after, last=False):
    n = len(plan)
    whole = lambda a: pl.BlockSpec(a.shape, lambda i: (0, 0))
    columns = pl.BlockSpec((SHARD, 512), lambda i: (0, base + i))
    out_columns = pl.BlockSpec((SHARD, 512), lambda i: (0, i))
    args = list(pieces) + [mine, got, cot, got_cot, after]
    in_specs = [whole(p) for p in pieces] + [columns, columns, whole(cot), whole(cot), TOKEN]
    if total is not None:
        args.append(total)
        in_specs.append(whole(total))
    wide = jax.ShapeDtypeStruct((SHARD, 512 * n), BF)
    if last:
        shapes = [wide, jax.ShapeDtypeStruct((SHARD, KV), F32), jax.ShapeDtypeStruct((SHARD, 1024), BF)]
        out_specs = [out_columns, whole(shapes[1]), whole(shapes[2]), TOKEN]
    else:
        shapes = [wide, wide, jax.ShapeDtypeStruct((512, KV), F32)]
        out_specs = [out_columns, out_columns, whole(shapes[2]), TOKEN]
    return pl.pallas_call(
        partial(products_kernel, plan=plan, n_pieces=len(pieces), first=total is None, last=last, scale=scale),
        grid=(n,),
        in_specs=in_specs,
        out_specs=out_specs,
        out_shape=shapes + [TOKEN_SHAPE],
        scratch_shapes=[pltpu.VMEM((512, KV), BF)],
        compiler_params=params(20),
        cost_estimate=cost(n * 8 * SHARD * 512 * 512, (n + 4) * MIB),
    )(*args)


def place_kernel(where, own, sib, *rest):
    out = rest[-1]
    y, core = where[Y], where[CORE]
    for k in range(2):
        y_at = lax.rem(y + k, 2)
        part = slice(k * SHARD, (k + 1) * SHARD)
        out[:, pl.ds(pl.multiple_of((y_at * 2 + core) * SHARD, SHARD), SHARD)] = own[:, part]
        out[:, pl.ds(pl.multiple_of((y_at * 2 + 1 - core) * SHARD, SHARD), SHARD)] = sib[:, part]


def place_last_kernel(where, own, sib, total, _, out, values, *, scale):
    place_kernel(where, own, sib, out)
    values[...] = ((total[...] + sib[:, 512:].astype(F32)) * scale).astype(BF)


def place(where, base, own, sib, into, total=None, scale=None):
    n = own.shape[1] // 512
    columns = pl.BlockSpec((SHARD, 512), lambda i, w: (0, i))
    held = pl.BlockSpec((SHARD, KV), lambda i, w: (0, 0))
    args, specs, aliases = [own, sib], [columns, columns], {}
    out_specs = [pl.BlockSpec((SHARD, 1024), lambda i, w: (0, w[base + i]))]
    shapes = [jax.ShapeDtypeStruct((SHARD, 8192), BF)]
    kernel = place_kernel
    if total is not None:
        kernel = partial(place_last_kernel, scale=scale)
        args.append(total)
        specs = [columns, pl.BlockSpec((SHARD, 1024), lambda i, w: (0, 0)), held]
        out_specs.append(held)
        shapes.append(jax.ShapeDtypeStruct((SHARD, KV), BF))
    if into is not None:
        args.append(into)
        specs.append(pl.BlockSpec(memory_space=pl.ANY))
        aliases = {len(args): 0}
    return pl.pallas_call(
        kernel,
        grid_spec=pltpu.PrefetchScalarGridSpec(
            num_scalar_prefetch=1, grid=(n,), in_specs=specs, out_specs=out_specs
        ),
        out_shape=shapes,
        input_output_aliases=aliases,
        compiler_params=params(8),
        cost_estimate=cost(0, n * MIB),
    )(where, *args)


def moved_kernel(local, from_y, su, sd, yf, momentum, moved, short):
    def add(*parts):
        total = parts[0].astype(F32)
        for part in parts[1:]:
            total = total + part.astype(F32)
        return total.T

    low = add(local[0:KV, :], from_y[...], su[0:KV, :], sd[0:KV, :])
    high = add(local[KV : 2 * KV, :], su[KV:, :], sd[KV:, :], yf[...])
    new_low = 0.9 * momentum[0:HALF, :] + low
    new_high = 0.9 * momentum[HALF:, :] + high
    moved[0:HALF, :] = new_low
    moved[HALF:, :] = new_high
    short[0:HALF, :] = new_low.astype(BF)
    short[HALF:, :] = new_high.astype(BF)


def move(local, from_y, su, sd, yf, momentum):
    whole = lambda rows, cols, index=0: pl.BlockSpec((rows, cols), lambda i: (index, 0))
    return pl.pallas_call(
        moved_kernel,
        grid=(1,),
        in_specs=[
            whole(3 * KV, HALF, Z - 1),
            whole(KV, HALF, 4),
            whole(2 * KV, HALF),
            whole(2 * KV, HALF),
            whole(KV, HALF),
            whole(SHARD, KV),
        ],
        out_specs=[whole(SHARD, KV), whole(SHARD, KV)],
        out_shape=[jax.ShapeDtypeStruct((SHARD, KV), F32), jax.ShapeDtypeStruct((SHARD, KV), BF)],
        compiler_params=params(16),
        cost_estimate=cost(0, 3 * MIB),
    )(local, from_y, su, sd, yf, momentum)


def average_kernel(where, rate, weight, moved, other_w, found, new_w, new_m):
    def step(given, by):
        return (given.astype(F32) - rate[0] * by).astype(BF).astype(F32)

    other_m = found[0][...]
    for bit in range(1, len(found)):
        other_m = jnp.where(where[PICK] == bit, found[bit][...], other_m)
    other_m = other_m.astype(F32)
    new_m[...] = (moved[...] + other_m) * 0.5
    new_w[...] = ((step(weight[...], moved[...]) + step(other_w[...], other_m)) * 0.5).astype(BF)


def average(where, rate, weight, moved, other_w, found):
    def kernel(where, rate, weight, moved, other_w, *rest):
        average_kernel(where, rate, weight, moved, other_w, rest[:-2], *rest[-2:])

    rows = pl.BlockSpec((HALF, KV), lambda i, *_: (i, 0))
    return pl.pallas_call(
        kernel,
        grid_spec=pltpu.PrefetchScalarGridSpec(
            num_scalar_prefetch=2,
            grid=(SHARD // HALF,),
            in_specs=[rows] * (3 + len(found)),
            out_specs=[rows, rows],
        ),
        out_shape=[jax.ShapeDtypeStruct((SHARD, KV), BF), jax.ShapeDtypeStruct((SHARD, KV), F32)],
        compiler_params=params(8),
        cost_estimate=cost(0, 3 * MIB),
    )(where, rate, weight, moved, other_w, *found)


def per_device(activations, weights, momentum, cotangent, step_index):
    acts, cot, w = activations[0], cotangent[0], weights[0]
    scale = 1.0 / (8192.0**0.5)
    me = lax.axis_index("fsdp")
    z, y, core = me // 4, (me // 2) % 2, me % 2

    bits = lax.axis_size("rep").bit_length() - 1
    step_float = step_index.astype(F32)
    rate = 0.1 * (0.5 + 0.5 * jnp.cos(jnp.float32(3.141592653589793) * step_float / 1000.0))
    where = jnp.stack([(z + d + Z) % Z for d in ORDER] + [y, core, step_index[0] % bits]).astype(jnp.int32)

    found = [from_partner(w, bit=bit) for bit in range(bits)]
    other_w, t_w = choose(where, found)

    u1, d1, y0 = up(w), down(w), y_swap(w)

    mine, give = prep(where, rate, acts)
    got, got_cot = core_swap(give), core_swap(cot)

    to_y0, to_y1, to_y2, local, t_part = partials(mine, got, cot, got_cot, scale)

    pay_u, pay_d, pay_y, _ = combine(
        [u1, d1, y0],
        [
            [[(0, HALF, HALF)], [(0, 0, HALF)], [(2, HALF, HALF)]],
            [[(1, 0, SHARD)], [(2, HALF, HALF)]],
            [[(0, 0, HALF)], [(1, 0, HALF)]],
        ]
    )
    u2, d2, y1 = up(pay_u), down(pay_d), y_swap(pay_y)
    from_y0, from_y1, from_y2 = y_swap(to_y0), y_swap(to_y1), y_swap(to_y2)

    def loc(i):
        return (local, 3 * KV, i)

    own, own_high, other = 0, KV, 2 * KV
    pay_u, pay_d, t_s1 = combine(
        [loc(0), loc(1), loc(2), from_y0],
        [
            [[(0, own, KV), (3, 0, KV)], [(1, other, KV)]],
            [[(0, own_high, KV), (3, KV, KV)], [(2, other, KV)]],
        ],
    )
    su1, sd1 = up(pay_u), down(pay_d)

    pay_y, _ = combine([u2, d2], [[[(0, HALF, HALF)], [(1, 0, HALF)]]])
    u3, d3, y2 = up(u2), down(d2), y_swap(pay_y)

    total = None
    ing1, give1, total, t_g1 = products(
        5,
        (
            ((1, 0, SHARD), (3, HALF, HALF), (5, 2 * HALF, HALF)),
            ((0, 0, SHARD), (3, 0, HALF), (4, 2 * HALF, HALF)),
            ((6, 0, SHARD), (2, 0, SHARD)),
        ),
        (u1, d1, y0, y1, u2, d2, w),
        mine, got, cot, got_cot, None, scale, t_part,
    )
    got1 = core_swap(give1)

    pay_u, pay_d, t_s2 = combine(
        [loc(1), loc(2), loc(3), loc(4), (from_y1, KV, 0), (from_y1, KV, 1), su1, sd1],
        [
            [[(0, own, KV), (4, 0, KV), (6, 0, KV)], [(0, own_high, KV)], [(2, other, KV), (6, KV, KV)]],
            [[(1, own, KV), (5, 0, KV)], [(1, own_high, KV), (7, 0, KV)], [(3, other, KV), (7, KV, KV)]],
        ],
    )
    su2, sd2 = up(pay_u), down(pay_d)

    pay_u, pay_d, pay_y, _ = combine(
        [u3, d3],
        [[[(0, HALF, SHARD)]], [[(1, HALF, SHARD)]], [[(0, HALF, HALF)], [(1, 0, HALF)]]]
    )
    u4, d4, y3 = up(pay_u), down(pay_d), y_swap(pay_y)
    ing2, give2, total, t_g2 = products(
        3,
        (
            ((1, 0, SHARD), (2, HALF, HALF), (4, SHARD, HALF)),
            ((0, HALF, HALF), (0, 0, HALF), (2, 0, HALF), (3, SHARD, HALF)),
        ),
        (u2, d2, y2, u3, d3),
        mine, got, cot, got_cot, total, scale, t_part,
    )
    got2 = core_swap(give2)

    def third(own_at, y_at, other_at, got_at):
        return [
            [(own_at, own, KV), (y_at, 0, KV), (got_at, 0, KV)],
            [(own_at, own_high, KV), (got_at, KV, KV)],
            [(other_at, other, KV), (got_at, 2 * KV, KV)],
        ]

    pay_u, pay_d, t_s3 = combine(
        [loc(3), loc(4), loc(5), loc(6), (from_y2, KV, 0), (from_y2, KV, 1), su2, sd2],
        [third(0, 4, 2, 6), third(1, 5, 3, 7)],
        after=(t_w,),
    )
    su3, sd3 = up(pay_u), down(pay_d)

    pay_u, pay_d, pay_y, t_s4 = combine(
        [loc(5), loc(6), loc(7), (from_y2, KV, 2), (from_y2, KV, 3), su3, sd3],
        [
            [[(0, own, KV), (3, 0, KV), (5, 0, KV)], [(0, own_high, KV), (5, KV, KV)]],
            [[(1, own, KV), (4, 0, KV), (6, 0, KV)], [(1, own_high, KV), (6, KV, KV)]],
            [[(2, other, KV), (5, 2 * KV, KV), (6, 2 * KV, KV)]],
        ]
    )
    su4, sd4, yf = up(pay_u), down(pay_d), y_swap(pay_y)

    pay_y, _ = combine([u4, d4], [[[(0, 0, HALF)], [(1, 0, HALF)]]])
    y4 = y_swap(pay_y)
    ing3, give3, total, t_g3 = products(
        1,
        (
            ((1, 0, SHARD), (2, HALF, HALF), (4, HALF, HALF)),
            ((0, HALF, HALF), (0, 0, HALF), (2, 0, HALF), (3, HALF, HALF)),
        ),
        (u3, d3, y3, u4, d4),
        mine, got, cot, got_cot, total, scale, t_part,
    )
    got3 = core_swap(give3)

    ing4, total, tail, _ = products(
        0,
        (((0, 0, HALF), (1, 0, HALF), (2, 0, SHARD)),),
        (u4, d4, y4),
        mine, got, cot, got_cot, total, scale, t_part, last=True,
    )
    got4 = core_swap(tail)

    moved, short = move(local, from_y2, su4, sd4, yf, momentum[0])
    found = [from_partner(short, bit=bit) for bit in range(bits)]
    new_w, new_m = average(where, rate, w, moved, other_w, found)

    (ingrad,) = place(where, 5, ing1, got1, None)
    (ingrad,) = place(where, 3, ing2, got2, ingrad)
    (ingrad,) = place(where, 1, ing3, got3, ingrad)
    ingrad, values = place(where, 0, ing4, got4, ingrad, total, scale)
    return (values[None], ingrad[None], new_w[None], new_m[None])


def solution(mesh):
    rows = P("rep", "fsdp", None)
    return jax.shard_map(
        per_device,
        mesh=mesh,
        in_specs=(rows, rows, rows, rows, P()),
        out_specs=(rows, rows, rows, rows),
        check_vma=False,
    )
```
